512 devices in a mesh: grp: 16 (over z), dev: 32 (over y, x, core).
Axes of the slice: x: 4, y: 4, z: 16, core: 2. Of those that a mesh axis runs over, the one named last changes fastest.
Arguments:
- records: bfloat16 [2048, 2, 2048], P(('grp', 'dev')), may hold values from -40 to 40
- partners: int32 [2048, 16], P(('grp', 'dev')), may hold values from 0 to 2047, as said below
- routes: int32 [2048, 2], P(('grp', 'dev')), may hold values from 0 to 15, all different within a row; in each aligned block of 4 rows (0 to 3, 4 to 7, ...) at most 2 rows name the same one
Outputs:
- near_corr: bfloat16 [2048, 16, 2048], P(('grp', 'dev'))
- far_corr: bfloat16 [16, 32, 32, 4, 2048], P('grp', 'dev')
The draws below stay inside these ranges and needn't reach their ends.
Inputs may be any that keep to these rules, and one draw needn't show every extreme that they name: partners[c, q] lies in the same segment of 128 channels as c, differs from c, and at most 16 channels away; every channel has partners exactly 16 below or above it. `routes`: each channel names 2 different groups; of the 4 channels of one device at most 2 name the same group, and some device reaches 2.
All inputs are finite; a program needn't handle non-finite values.
Results may differ from the reference program's by a relative error of at most 0.0081.
Values may be sent and summed in bfloat16 or wider, within the bound.
No kernel may reach another device: no remote copies, remote signals or barrier semaphores. Data moves between devices by JAX's collectives and lax.ppermute only.
A program may use at most 64 MiB of HBM per device.

```python
import math
import jax
import jax.numpy as jnp
import numpy as np
from jax import lax

C_DEV = 4
W = 2
NT = 2048
Q = 16
TOPR = 2
MAXOFF = 16
GROUP_CH = 128
CH = 2048
CAP = 2
SLOTS = 32
N_GRP = 16
N_DEV = 32


def draw_records(key, part):
    key = jax.random.fold_in(key, 11)
    noise_key, scale_key, amp_key, bin_key, phase_key = jax.random.split(key, 5)
    sample_index = jnp.arange(NT, dtype=jnp.int32)
    tone_bins = jax.random.randint(bin_key, (CH, W, 3), 1, NT // 2)
    tone_phase = jax.random.uniform(phase_key, (CH, W, 3), jnp.float32, 0.0, 2.0 * math.pi)
    tone_amp = jax.random.uniform(amp_key, (CH, W, 3), jnp.float32, 0.2, 1.0)
    angles = (tone_bins[..., None] * sample_index % NT).astype(jnp.float32) * (2.0 * math.pi / NT)
    tones = jnp.sum(tone_amp[..., None] * jnp.cos(angles + tone_phase[..., None]), axis=2)
    noise_part = jnp.clip(jax.random.normal(noise_key, (CH, W, NT), jnp.float32), -6.0, 6.0)
    spread = jnp.exp(jax.random.uniform(scale_key, (CH, W, 1), jnp.float32, -1.2, 1.2))
    return (spread * (noise_part + tones)).astype(jnp.bfloat16)


def draw_partners(key, part):
    key = jax.random.fold_in(key, 23)
    size_key, side_key = jax.random.split(key)
    channel = jnp.arange(CH, dtype=jnp.int32)[:, None]
    column = jnp.arange(Q, dtype=jnp.int32)[None, :]
    magnitude = jax.random.randint(size_key, (CH, Q), 1, MAXOFF + 1)
    signs = 2 * jax.random.randint(side_key, (CH, Q), 0, 2) - 1
    magnitude = jnp.where(column < 2, MAXOFF, magnitude)
    signs = jnp.where(column == 0, -1, jnp.where(column == 1, 1, signs))
    offset = magnitude * signs
    group_lo = channel // GROUP_CH * GROUP_CH
    target = channel + offset
    inside = (target >= group_lo) & (target < group_lo + GROUP_CH)
    return jnp.where(inside, target, channel - offset).astype(jnp.int32)


def routed_block(key, own, number, rows, count, top, bound, slope):
    order = jax.random.permutation(key, count)
    heavy_load, ordinary = shares(count, rows * top, bound, slope, True), shares(count, rows * top, bound, slope, False)
    places = jnp.arange(count)

    def named(sizes, rotation):
        used = int((sizes > 0).sum())
        fixed = max(1, used // 4)
        passed = fixed + (places - fixed + rotation * (used - fixed)) % max(1, count - fixed)
        return jnp.zeros((count,), jnp.int32).at[order[jnp.where(places < fixed, places, passed)]].set(jnp.asarray(sizes, jnp.int32))

    sizes = jnp.where(number % 4 == 0, named(heavy_load, number // 4), named(ordinary, number - number // 4 - 1))
    mixed = jax.random.permutation(jax.random.fold_in(own, 3), count)
    giver, taker = mixed[0:count // 2 * 2:2], mixed[1:count // 2 * 2:2]
    margin = jnp.minimum(sizes[giver] - 1, bound - sizes[taker]) // 2
    margin = jnp.where((giver == order[0]) | (taker == order[0]) | (sizes[taker] == 0), 0, jnp.maximum(margin, 0))
    passed = jax.random.randint(jax.random.fold_in(own, 4), (count // 2,), 0, 1 << 20) % (margin + 1)
    sizes = sizes.at[giver].add(-passed).at[taker].add(passed)
    members = jnp.searchsorted(jnp.cumsum(sizes), jnp.arange(rows * top), side="right").astype(jnp.int32)
    listing = members.reshape(top, rows).T
    listing = listing[jax.random.permutation(jax.random.fold_in(own, 1), rows)]
    rotation = jax.random.randint(jax.random.fold_in(own, 2), (rows, 1), 0, top)
    return jnp.take_along_axis(listing, (jnp.arange(top)[None, :] + rotation) % top, axis=1)


def shares(number_of, total, bound, lean, full):
    weights = [(1 << 20) // math.isqrt(rank ** lean) + 1 for rank in range(1, number_of + 1)]
    largest = bound if full else min(bound, max(-(-total // number_of), total * weights[0] // sum(weights)))
    least = 1 if total - largest >= number_of - 1 else 0
    holding, spare = [largest] + [least] * (number_of - 1), total - largest - least * (number_of - 1)
    while spare > 0:
        candidates = [i for i in range(1, number_of) if holding[i] < largest] or [i for i in range(1, number_of) if holding[i] < bound]
        pool, budget = sum([weights[i] for i in candidates]), spare
        for i in candidates:
            more = min(bound - holding[i], max(1, budget * weights[i] // pool), spare)
            holding[i] = holding[i] + more
            spare = spare - more
    return np.array(holding)


def setup_inputs(seed: int = 0) -> dict:
    key_list = jax.random.split(jax.random.key(seed), 4)
    records = draw_records(jax.random.fold_in(key_list[3], 71), 0)
    partners = draw_partners(jax.random.fold_in(key_list[3], 71), 0)
    routes_keys = jax.random.split(jax.random.fold_in(key_list[2], 1), CH // C_DEV)
    routes_turns = jax.random.permutation(jax.random.fold_in(key_list[2], 3), CH // C_DEV)
    routes = jax.vmap(lambda own, number: routed_block(jax.random.fold_in(key_list[2], 2), own, number, C_DEV, N_GRP, TOPR, CAP, 2))(routes_keys, routes_turns).reshape((CH, TOPR))
    return dict(records=records, partners=partners, routes=routes)


def tables(length):
    lag_index = jnp.arange(length, dtype=jnp.int32)
    bin_index = jnp.arange(length // 2, dtype=jnp.int32)
    angles = (lag_index[:, None] * bin_index[None, :] % length).astype(jnp.float32) * (2.0 * math.pi / length)
    return (jnp.cos(angles).astype(jnp.bfloat16), (-jnp.sin(angles)).astype(jnp.bfloat16))

def forward(data_rows, cos_t, sin_t):
    real_part = jnp.dot(data_rows, cos_t, preferred_element_type=jnp.float32)
    imag_part = jnp.dot(data_rows, sin_t, preferred_element_type=jnp.float32)
    return jnp.concatenate([real_part, imag_part], axis=1)

def whiten(spectra):
    half_len = spectra.shape[1] // 2
    real_part = spectra[:, :half_len]
    imag_part = spectra[:, half_len:]
    energy = real_part * real_part + imag_part * imag_part
    mean_level = lax.optimization_barrier(jnp.mean(energy, axis=1, keepdims=True))
    scale_by = jnp.sqrt(energy + 0.1 * mean_level + 1e-06)
    return jnp.concatenate([real_part / scale_by, imag_part / scale_by], axis=1).astype(jnp.bfloat16)

def cross_spectra(left_rows, right_rows):
    half_len = left_rows.shape[2] // 2
    left_f = left_rows.astype(jnp.float32)
    right_f = right_rows.astype(jnp.float32)
    left_real, left_imag = (left_f[:, :, :half_len], left_f[:, :, half_len:])
    right_real, right_imag = (right_f[:, :, :half_len], right_f[:, :, half_len:])
    real_sum = lax.optimization_barrier(jnp.sum(left_real * right_real + left_imag * right_imag, axis=1))
    imag_sum = lax.optimization_barrier(jnp.sum(left_imag * right_real - left_real * right_imag, axis=1))
    return jnp.concatenate([real_sum, imag_sum], axis=1).astype(jnp.bfloat16)

def inverse(spectra, cos_t, sin_t, windows):
    half_len = spectra.shape[1] // 2
    lagged = jnp.dot(spectra[:, :half_len], cos_t.T, preferred_element_type=jnp.float32)
    lagged = lagged + jnp.dot(spectra[:, half_len:], sin_t.T, preferred_element_type=jnp.float32)
    return (lagged * (1.0 / (windows * math.sqrt(half_len)))).astype(jnp.bfloat16)

def reference(records, partners, routes):
    cos_t, sin_t = tables(NT)
    whitened = whiten(forward(records.reshape(CH * W, NT), cos_t, sin_t)).reshape(CH, W, NT)
    devices = N_GRP * N_DEV
    white_dev = whitened.reshape(devices, C_DEV, W * NT)
    routes_dev = routes.reshape(devices, C_DEV, TOPR)

    def build_send(inputs):
        own_rows, own_routes = inputs
        targets = jnp.arange(N_GRP, dtype=jnp.int32)
        routed = jnp.any(own_routes[:, :, None] == targets[None, None, :], axis=1)
        counts = routed.astype(jnp.int32)
        slot_of = jnp.cumsum(counts, axis=0) - counts
        picker = (routed[:, :, None] & (slot_of[:, :, None] == jnp.arange(CAP, dtype=jnp.int32)[None, None, :])).astype(jnp.float32)
        return jnp.einsum('chk,cl->hkl', picker, own_rows.astype(jnp.float32)).astype(jnp.bfloat16)
    sent_rows = lax.map(build_send, (white_dev, routes_dev))
    sent_rows = sent_rows.reshape(N_GRP, N_DEV, N_GRP, CAP, W * NT)
    received = jnp.transpose(sent_rows, (2, 1, 0, 3, 4)).reshape(devices, SLOTS, W, NT)
    partner_dev = partners.reshape(devices, C_DEV * Q)

    def per_device(inputs):
        own_rows, partner_ids, far_rows = inputs
        own_rows = own_rows.reshape(C_DEV, W, NT)
        partner_rows = jnp.take(whitened, partner_ids, axis=0)
        near_spec = cross_spectra(jnp.repeat(own_rows, Q, axis=0), partner_rows)
        far_spec = cross_spectra(jnp.repeat(far_rows, C_DEV, axis=0), jnp.tile(own_rows, (SLOTS, 1, 1)))
        lagged = inverse(jnp.concatenate([near_spec, far_spec], axis=0), cos_t, sin_t, W)
        return (lagged[:C_DEV * Q], lagged[C_DEV * Q:])
    near_out, far_out = lax.map(per_device, (white_dev, partner_dev, received))
    near_corr = near_out.reshape(CH, Q, NT)
    far_corr = far_out.reshape(N_GRP, N_DEV, SLOTS, C_DEV, NT)
    return (near_corr, far_corr)
```

```python
import math

import jax
import jax.numpy as jnp
import numpy as np
from jax import lax
from jax.experimental import pallas as pl
from jax.experimental.pallas import tpu as pltpu
from jax.sharding import PartitionSpec as P

NT = 2048
BINS = 1024
LANES = 128
ROWS = 32
C = math.sqrt(0.5)
COLS = ((0, 128), (256, 384), (512, 768), (640, 896), (1024, 1280), (1152, 1408), (1536, 1792), (1664, 1920))
F32, BF16 = jnp.float32, jnp.bfloat16


def make_tables():
    b = np.arange(256)
    k = np.arange(128)

    def trig(bins):
        angle = (b[:, None] * bins[None, :]) % NT * (2.0 * np.pi / NT)
        return np.cos(angle), np.sin(angle)

    tiles = [np.concatenate([cos, -sin], axis=1) for cos, sin in (trig(8 * k), trig(8 * k + 4))]
    for r in (2, 1, 3):
        tiles += trig(np.concatenate([8 * k + r, -(8 * k + 8 - r)]))

    def stacked(tiles):
        cut = [tile[:, lo : lo + LANES] for tile in tiles for lo in (0, LANES)]
        return np.concatenate(cut, axis=0).astype(np.float32).astype(jnp.bfloat16)

    return stacked(tiles + [tile.T for tile in tiles])


TILES = 8
VMEM_LIMIT = 60 * 1024 * 1024


def dot(a, b):
    return jnp.dot(a, b, preferred_element_type=F32)


def fetch(pairs, sems):
    moves = [pltpu.make_async_copy(src, dst, sems.at[m]) for m, (src, dst) in enumerate(pairs)]
    for move in moves:
        move.start()
    return moves


def tile(table_ref, m):
    return jnp.concatenate([table_ref[pl.ds(512 * m, 256), :], table_ref[pl.ds(512 * m + 256, 256), :]], axis=1)


def products(one_ref, two_ref, y_ref, n, table_ref, first, sign):
    for m in range(2):
        y_ref[0:n, 256 * m : 256 * (m + 1)] = dot(one_ref[m], tile(table_ref, first + m))
    for m in range(3):
        c = dot(two_ref[m], tile(table_ref, first + 2 + 2 * m))
        s = dot(two_ref[m], tile(table_ref, first + 3 + 2 * m))
        col = 512 * (m + 1)
        re, im = (c[:n] + s[n:], c[n:] - s[:n]) if sign == 1 else (c[:n] - s[n:], c[n:] + s[:n])
        y_ref[0:n, col : col + 256] = re
        y_ref[0:n, col + 256 : col + 512] = im


def select_kernel(routes_hbm, own_hbm, out_ref, routes_ref, own_ref, sems):
    for move in fetch([(routes_hbm, routes_ref), (own_hbm, own_ref)], sems):
        move.wait()
    for h in range(16):
        hit = [(routes_ref[0, i] == h) | (routes_ref[1, i] == h) for i in range(4)]
        count = sum(x.astype(jnp.int32) for x in hit)
        first = jnp.where(hit[0], 0, jnp.where(hit[1], 1, jnp.where(hit[2], 2, 3)))
        last = jnp.where(hit[3], 3, jnp.where(hit[2], 2, jnp.where(hit[1], 1, 0)))
        for k, pick in ((0, first), (1, last)):
            rows = own_ref[pl.ds(pl.multiple_of(pick * ROWS, ROWS), ROWS), :]
            out_ref[pl.ds((2 * h + k) * ROWS, ROWS), :] = jnp.where(count > k, rows, jnp.zeros_like(rows))


def spread(x_ref, stride, start, blk_ref, count):
    for c in range(count):
        x_ref[pl.ds((start + c) * stride, ROWS), :] = blk_ref[pl.ds(c * ROWS, ROWS), :].astype(F32)


def forward(x_ref, stride, n, one_ref, two_ref, z_ref, table_ref, move):
    for w in range(2):
        for half in range(2):
            x = [x_ref[pl.ds(2 * (2 * a + half) + w, n, stride=stride), :] for a in range(8)]
            s = [x[a] + x[a + 4] for a in range(4)]
            d = [x[a] - x[a + 4] for a in range(4)]
            even, odd = s[0] + s[2], s[1] + s[3]
            diff, summ = C * (d[1] - d[3]), C * (d[1] + d[3])
            lanes = pl.ds(half * LANES, LANES)
            for m, part in enumerate((even + odd, even - odd)):
                one_ref[m, pl.ds(w * n, n), lanes] = part.astype(BF16)
            for m, parts in enumerate(
                ((s[0] - s[2], s[3] - s[1]), (d[0] + diff, -d[2] - summ), (d[0] - diff, d[2] - summ))
            ):
                for k, part in enumerate(parts):
                    two_ref[m, pl.ds((2 * k + w) * n, n), lanes] = part.astype(BF16)
    move.wait()
    products(one_ref, two_ref, z_ref, 2 * n, table_ref, 0, 1)
    total = None
    for re, im in COLS:
        zr, zi = z_ref[0 : 2 * n, re : re + LANES], z_ref[0 : 2 * n, im : im + LANES]
        energy = zr * zr + zi * zi
        total = energy if total is None else total + energy
    return jnp.sum(total, axis=1, keepdims=True) * (1.0 / BINS)


def whitened(z_ref, level, re, im):
    n = level.shape[0]
    zr, zi = z_ref[0:n, re : re + LANES], z_ref[0:n, im : im + LANES]
    scale = lax.rsqrt(zr * zr + zi * zi + level)
    return zr * scale, zi * scale


def put(one_ref, two_ref, chunk, lo, sr, si):
    n = sr.shape[0]
    sr, si = (sr * (1.0 / 64)).astype(BF16), (si * (1.0 / 64)).astype(BF16)
    if chunk < 2:
        one_ref[chunk, pl.ds(lo, n), 0:LANES] = sr
        one_ref[chunk, pl.ds(lo, n), LANES : 2 * LANES] = si
    else:
        rows = two_ref.shape[1] // 2
        m, lanes = (chunk - 2) // 2, pl.ds(chunk % 2 * LANES, LANES)
        two_ref[m, pl.ds(lo, n), lanes] = sr
        two_ref[m, pl.ds(rows + lo, n), lanes] = si


def lags(h_ref, lo, n, half):
    p0, p4, a2, b2, a1, b1, a3, b3 = (
        h_ref[lo : lo + n, 256 * m + half * LANES : 256 * m + (half + 1) * LANES] for m in range(8)
    )
    even, odd = p0 + p4, p0 - p4
    plus, minus = even + a2, even - a2
    a13, b31 = a1 + a3, b3 - b1
    low, high = odd - b2, odd + b2
    t1, t3 = C * (a1 - b1 - a3 - b3), C * (a3 - b3 - a1 - b1)
    return (plus + a13, low + t1, minus + b31, high + t3, plus - a13, low - t1, minus - b31, high - t3)


NEAR, FAR, N = 48, 32, 80
STRIDE = 40
PAIRS, SLOT = 64 + 4 * FAR, 72
GROUP = 8


def picked(dev, partners_ref):
    core = dev % 2
    col = lax.broadcasted_iota(jnp.int32, (64, NEAR), 1)
    row = lax.broadcasted_iota(jnp.int32, (64, NEAR), 0)
    wanted = jnp.zeros((64, NEAR), jnp.int32)
    for c in range(4):
        for q in range(16):
            wanted = jnp.where(row == c * 16 + q, partners_ref[c, q] & 127, wanted)
    block = col // 8
    step = jnp.where(block == 1, -1, jnp.where(block == 2, -2, jnp.where(block == 3, 1, jnp.where(block == 4, 2, 0))))
    flip = jnp.where(block >= 3, 1, 0)
    in_core = (core + flip + (col // 4) % 2) % 2
    ids = 8 * (dev // 2 + (1 - 2 * core) * step) + in_core * 4 + col % 4
    ids = jnp.where(block < 5, ids, -1)
    return jnp.where(wanted == ids, 1.0, 0.0).astype(BF16)


def correlate_kernel(dev_ref, partners_hbm, *refs):
    near_hbm, (recv_hbm, table_hbm, near_out, far_out), refs = refs[:5], refs[5:9], refs[9:]
    near_refs, (recv_ref, table_ref, partners_ref), refs = refs[:5], refs[5:8], refs[8:]
    x_ref, u1_ref, u2_ref, z_ref, w_ref, p_ref, s1_ref, s2_ref, h_ref, o_ref, near_ref, far_ref, sems, out_sems = refs
    half = 512 * TILES
    moves = fetch(
        [
            (table_hbm.at[pl.ds(0, half), :], table_ref.at[pl.ds(0, half), :]),
            *zip(near_hbm, near_refs),
            (recv_hbm, recv_ref),
            (partners_hbm, partners_ref),
            (table_hbm.at[pl.ds(half, half), :], table_ref.at[pl.ds(half, half), :]),
        ],
        sems,
    )
    x_ref[pl.ds(40 * STRIDE, 8 * STRIDE), :] = jnp.zeros((8 * STRIDE, LANES), F32)
    for move in moves[1:8]:
        move.wait()
    for m, ref in enumerate(near_refs):
        spread(x_ref, STRIDE, 8 * m, ref, 8)
    spread(x_ref, STRIDE, NEAR, recv_ref, FAR)
    level = 0.1 * forward(x_ref, STRIDE, N, u1_ref, u2_ref, z_ref, table_ref, moves[0]) + 1e-6
    for chunk, (re, im) in enumerate(COLS):
        wr, wi = whitened(z_ref, level, re, im)
        for w in range(2):
            w_ref[w, :, re : re + LANES] = wr[w * N : w * N + NEAR].astype(BF16)
            w_ref[w, :, im : im + LANES] = wi[w * N : w * N + NEAR].astype(BF16)
        for i in range(4):
            sr = si = 0.0
            for w in range(2):
                at = w * N + NEAR
                fr, fi = wr[at : at + FAR], wi[at : at + FAR]
                br, bi = wr[w * N + i : w * N + i + 1], wi[w * N + i : w * N + i + 1]
                sr = sr + (fr * br + fi * bi)
                si = si + (fi * br - fr * bi)
            put(s1_ref, s2_ref, chunk, 64 + i * FAR, sr, si)
    picker = picked(dev_ref[0], partners_ref)
    for w in range(2):
        p_ref[w] = dot(picker, w_ref[w])
    for chunk, (re, im) in enumerate(COLS):
        own = [[w_ref[w, 0:16, k : k + LANES].astype(F32) for k in (re, im)] for w in range(2)]
        for c in range(4):
            sr = si = 0.0
            for w in range(2):
                pr, pi = (p_ref[w, c * 16 : (c + 1) * 16, k : k + LANES] for k in (re, im))
                ar, ai = own[w][0][c : c + 1], own[w][1][c : c + 1]
                sr = sr + (ar * pr + ai * pi)
                si = si + (ai * pr - ar * pi)
            put(s1_ref, s2_ref, chunk, c * 16, sr, si)
    moves[8].wait()
    products(s1_ref, s2_ref, h_ref, PAIRS, table_ref, TILES, -1)
    for lo in range(0, 64, 16):
        for part in range(2):
            for a, lag in enumerate(lags(h_ref, lo, 16, part)):
                at = 256 * a + LANES * part
                near_ref[lo : lo + 16, at : at + LANES] = lag.astype(BF16)
    outs = [pltpu.make_async_copy(near_ref, near_out, out_sems.at[0])]
    outs[0].start()
    for g in range(FAR // GROUP):
        for i in range(4):
            for part in range(2):
                for a, lag in enumerate(lags(h_ref, 64 + i * FAR + g * GROUP, GROUP, part)):
                    o_ref[pl.ds(g * GROUP * SLOT + (2 * a + part) * 4 + i, GROUP, stride=SLOT), :] = lag
        for s in range(g * GROUP, (g + 1) * GROUP):
            far_ref[pl.ds(s * 64, 64), :] = o_ref[pl.ds(s * SLOT, 64), :].astype(BF16)
        rows = pl.ds(g * GROUP * 64, GROUP * 64)
        outs.append(pltpu.make_async_copy(far_ref.at[rows, :], far_out.at[rows, :], out_sems.at[1 + g]))
        outs[-1].start()
    for out in outs:
        out.wait()


def vmem():
    return pl.BlockSpec(memory_space=pltpu.VMEM)


def smem():
    return pl.BlockSpec(memory_space=pltpu.SMEM)


def hbm():
    return pl.BlockSpec(memory_space=pltpu.HBM)


def like(*shape):
    return jax.ShapeDtypeStruct(shape, BF16)


def shards(records, partners, routes):
    table = jnp.asarray(make_tables())
    members = lax.axis_size("dev")
    swap = [(d, d ^ 1) for d in range(members)]

    def toward(chips):
        pairs = [(d, d + (2 * chips if d % 2 == 0 else -2 * chips)) for d in range(members)]
        return [(s, t) for s, t in pairs if 0 <= t < members]

    raw = records.reshape(4, 2, 16, LANES).transpose(0, 2, 1, 3).reshape(4 * ROWS, LANES)
    outgoing = pl.pallas_call(
        select_kernel,
        out_shape=like(32 * ROWS, LANES),
        in_specs=[hbm(), hbm()],
        out_specs=vmem(),
        scratch_shapes=[
            pltpu.SMEM((2, 4), jnp.int32),
            pltpu.VMEM((4 * ROWS, LANES), BF16),
            pltpu.SemaphoreType.DMA((2,)),
        ],
        name="select",
    )(routes.T, raw)
    other = lax.ppermute(raw, "dev", swap)
    outgoing, other = lax.optimization_barrier((outgoing, other))
    arrived = lax.all_to_all(outgoing.reshape(16, 2 * ROWS, LANES), "grp", 0, 0, tiled=True).reshape(32 * ROWS, LANES)

    chip = jnp.concatenate([raw, other], axis=0)
    one_side = lax.ppermute(chip, "dev", toward(1))
    two_side = lax.ppermute(chip, "dev", toward(2))
    one_far = lax.ppermute(one_side, "dev", swap)
    two_far = lax.ppermute(two_side, "dev", swap)
    dev = lax.axis_index("dev").astype(jnp.int32).reshape(1)
    blocks = (chip, one_side, two_side, one_far, two_far)
    near, far = pl.pallas_call(
        correlate_kernel,
        out_shape=(like(64, NT), like(64 * FAR, LANES)),
        in_specs=[smem()] + [hbm()] * 8,
        out_specs=(hbm(), hbm()),
        scratch_shapes=[pltpu.VMEM(x.shape, BF16) for x in (*blocks, arrived, table)]
        + [
            pltpu.SMEM((4, 16), jnp.int32),
            pltpu.VMEM((N * STRIDE, LANES), F32),
            pltpu.VMEM((2, 2 * N, 256), BF16),
            pltpu.VMEM((3, 4 * N, 256), BF16),
            pltpu.VMEM((2 * N, NT), F32),
            pltpu.VMEM((2, NEAR, NT), BF16),
            pltpu.VMEM((2, 64, NT), F32),
            pltpu.VMEM((2, PAIRS, 256), BF16),
            pltpu.VMEM((3, 2 * PAIRS, 256), BF16),
            pltpu.VMEM((PAIRS, NT), F32),
            pltpu.VMEM((FAR * SLOT, LANES), F32),
            pltpu.VMEM((64, NT), BF16),
            pltpu.VMEM((64 * FAR, LANES), BF16),
            pltpu.SemaphoreType.DMA((9,)),
            pltpu.SemaphoreType.DMA((1 + FAR // GROUP,)),
        ],
        compiler_params=pltpu.CompilerParams(vmem_limit_bytes=VMEM_LIMIT),
        name="correlate",
    )(dev, partners, *blocks, arrived, table)
    far = far.reshape(32, 16, 4, LANES).transpose(0, 2, 1, 3).reshape(1, 1, 32, 4, NT)
    return (near.reshape(4, 16, NT), far)


def solution(mesh):
    placed = (P(("grp", "dev"), None, None), P(("grp", "dev"), None), P(("grp", "dev"), None))
    return jax.shard_map(
        shards,
        mesh=mesh,
        in_specs=placed,
        out_specs=(P(("grp", "dev"), None, None), P("grp", "dev", None, None, None)),
        check_vma=False,
    )
```

```python
import math

import jax
import jax.numpy as jnp
import numpy as np
from jax import lax
from jax.experimental import pallas as pl
from jax.experimental.pallas import tpu as pltpu
from jax.sharding import PartitionSpec as P

NT = 2048
BINS = 1024
LANES = 128
ROWS = 32
C = math.sqrt(0.5)
COLS = ((0, 128), (256, 384), (512, 768), (640, 896), (1024, 1280), (1152, 1408), (1536, 1792), (1664, 1920))
F32, BF16 = jnp.float32, jnp.bfloat16


def make_tables():
    b = np.arange(256)
    angle = b[:, None] * b[None, :] % 256 * (2.0 * np.pi / 256)
    blocks = [f(angle)[:, lo : lo + LANES] for f in (np.cos, np.sin) for lo in (0, LANES)]
    turn = np.array([2, 1, 3, 4])[:, None] * b[None, :] * (2.0 * np.pi / NT)
    twiddles = np.concatenate([np.cos(turn), np.sin(turn)], axis=0).astype(np.float32)
    return np.concatenate(blocks, axis=0).astype(np.float32).astype(jnp.bfloat16), twiddles


VMEM_LIMIT = 60 * 1024 * 1024


def dot(a, b):
    return jnp.dot(a, b, preferred_element_type=F32)


def fetch(pairs, sems):
    moves = [pltpu.make_async_copy(src, dst, sems.at[m]) for m, (src, dst) in enumerate(pairs)]
    for move in moves:
        move.start()
    return moves


def whole(table_ref):
    c0, c1, s0, s1 = (table_ref[pl.ds(256 * m, 256), :] for m in range(4))
    top = jnp.concatenate([c0, c1, -s0, -s1], axis=1)
    return jnp.concatenate([top, jnp.concatenate([s0, s1, c0, c1], axis=1)], axis=0)


def half(table_ref):
    c, s = table_ref[pl.ds(0, 256), :], table_ref[pl.ds(512, 256), :]
    return jnp.concatenate([jnp.concatenate([c, -s], axis=1), jnp.concatenate([s, c], axis=1)], axis=0)


def half_inverse(table_ref):
    c0, c1, s0, s1 = (table_ref[pl.ds(256 * m, LANES), :] for m in range(4))
    top = jnp.concatenate([c0, c1, -s0, -s1], axis=1)
    return jnp.concatenate([top, jnp.concatenate([s0, s1, c0, c1], axis=1)], axis=0)


def select_kernel(routes_hbm, own_hbm, out_ref, routes_ref, own_ref, sems):
    for move in fetch([(routes_hbm, routes_ref), (own_hbm, own_ref)], sems):
        move.wait()
    for h in range(16):
        hit = [(routes_ref[0, i] == h) | (routes_ref[1, i] == h) for i in range(4)]
        count = sum(x.astype(jnp.int32) for x in hit)
        first = jnp.where(hit[0], 0, jnp.where(hit[1], 1, jnp.where(hit[2], 2, 3)))
        last = jnp.where(hit[3], 3, jnp.where(hit[2], 2, jnp.where(hit[1], 1, 0)))
        for k, pick in ((0, first), (1, last)):
            rows = own_ref[pl.ds(pl.multiple_of(pick * ROWS, ROWS), ROWS), :]
            out_ref[pl.ds((2 * h + k) * ROWS, ROWS), :] = jnp.where(count > k, rows, jnp.zeros_like(rows))


def spread(x_ref, stride, start, blk_ref, count):
    for c in range(count):
        x_ref[pl.ds((start + c) * stride, ROWS), :] = blk_ref[pl.ds(c * ROWS, ROWS), :].astype(F32)


def forward(x_ref, stride, n, one_ref, four_ref, two_ref, z_ref, table_ref, tw_ref, moves):
    rows = 2 * n
    moves[1].wait()
    for part in range(2):
        lanes = pl.ds(part * LANES, LANES)
        lanes_im = pl.ds(256 + part * LANES, LANES)
        cos = [jnp.broadcast_to(tw_ref[m : m + 1, lanes], (n, LANES)) for m in range(4)]
        sin = [jnp.broadcast_to(tw_ref[m + 4 : m + 5, lanes], (n, LANES)) for m in range(4)]
        for w in range(2):
            x = [x_ref[pl.ds(2 * (2 * a + part) + w, n, stride=stride), :] for a in range(8)]
            s = [x[a] + x[a + 4] for a in range(4)]
            d = [x[a] - x[a + 4] for a in range(4)]
            even, odd = s[0] + s[2], s[1] + s[3]
            diff, summ = C * (d[1] - d[3]), C * (d[1] + d[3])
            one_ref[pl.ds(w * n, n), lanes] = (even + odd).astype(BF16)
            four = even - odd
            four_ref[pl.ds(w * n, n), lanes] = (four * cos[3]).astype(BF16)
            four_ref[pl.ds(w * n, n), lanes_im] = (-four * sin[3]).astype(BF16)
            for m, (re, im) in enumerate(
                ((s[0] - s[2], s[3] - s[1]), (d[0] + diff, -d[2] - summ), (d[0] - diff, d[2] - summ))
            ):
                two_ref[pl.ds(m * rows + w * n, n), lanes] = (re * cos[m] + im * sin[m]).astype(BF16)
                two_ref[pl.ds(m * rows + w * n, n), lanes_im] = (im * cos[m] - re * sin[m]).astype(BF16)
    moves[0].wait()
    table = half(table_ref)
    z_ref[:, 0:256] = dot(one_ref[...], table[0:256])
    z_ref[:, 256:512] = dot(four_ref[...], table)
    table = whole(table_ref)
    y = dot(two_ref[...], table)
    for m in range(3):
        z_ref[:, 512 * (m + 1) : 512 * (m + 2)] = y[m * rows : (m + 1) * rows]
    total = None
    for re, im in COLS:
        zr, zi = z_ref[:, re : re + LANES], z_ref[:, im : im + LANES]
        energy = zr * zr + zi * zi
        total = energy if total is None else total + energy
    return jnp.sum(total, axis=1, keepdims=True) * (1.0 / BINS)


def backward(one_ref, two_ref, h_ref, n, table_ref, tw_ref):
    table = half_inverse(table_ref)
    h_ref[:, 0:256] = dot(one_ref[pl.ds(0, n), :], table[:, 0:256])
    y = dot(one_ref[pl.ds(n, n), :], table)
    h_ref[:, 256:512] = y[:, 0:256] * tw_ref[3:4, :] + y[:, 256:512] * tw_ref[7:8, :]
    table = whole(table_ref)
    whole_y = dot(two_ref[...], table)
    for m in range(3):
        y = whole_y[m * n : (m + 1) * n]
        re, minus_im = y[:, 0:256], y[:, 256:512]
        cos, sin = tw_ref[m : m + 1, :], tw_ref[m + 4 : m + 5, :]
        col = 512 * (m + 1)
        h_ref[:, col : col + 256] = re * cos + minus_im * sin
        h_ref[:, col + 256 : col + 512] = re * sin - minus_im * cos


def whitened(z_ref, level, re, im):
    n = level.shape[0]
    zr, zi = z_ref[0:n, re : re + LANES], z_ref[0:n, im : im + LANES]
    scale = lax.rsqrt(zr * zr + zi * zi + level)
    return zr * scale, zi * scale


def put(one_ref, two_ref, chunk, lo, sr, si):
    n = sr.shape[0]
    sr, si = (sr * (1.0 / 64)).astype(BF16), (si * (1.0 / 64)).astype(BF16)
    if chunk < 2:
        rows = pl.ds(chunk * (one_ref.shape[0] // 2) + lo, n)
        one_ref[rows, 0:LANES] = sr
        one_ref[rows, LANES : 2 * LANES] = -si
    else:
        rows = pl.ds((chunk - 2) // 2 * (two_ref.shape[0] // 3) + lo, n)
        at = chunk % 2 * LANES
        two_ref[rows, at : at + LANES] = sr
        two_ref[rows, 256 + at : 256 + at + LANES] = -si


def lags(h_ref, lo, n, half):
    p0, p4, a2, b2, a1, b1, a3, b3 = (
        h_ref[lo : lo + n, 256 * m + half * LANES : 256 * m + (half + 1) * LANES] for m in range(8)
    )
    even, odd = p0 + p4, p0 - p4
    plus, minus = even + a2, even - a2
    a13, b31 = a1 + a3, b3 - b1
    low, high = odd - b2, odd + b2
    t1, t3 = C * (a1 - b1 - a3 - b3), C * (a3 - b3 - a1 - b1)
    return (plus + a13, low + t1, minus + b31, high + t3, plus - a13, low - t1, minus - b31, high - t3)


NEAR, FAR, N = 48, 32, 80
STRIDE = 40
PAIRS, SLOT = 64 + 4 * FAR, 72
GROUP = 8


def picked(dev, partners_ref):
    core = dev % 2
    col = lax.broadcasted_iota(jnp.int32, (64, NEAR), 1)
    row = lax.broadcasted_iota(jnp.int32, (64, NEAR), 0)
    wanted = jnp.zeros((64, NEAR), jnp.int32)
    for c in range(4):
        for q in range(16):
            wanted = jnp.where(row == c * 16 + q, partners_ref[c, q] & 127, wanted)
    block = col // 8
    step = jnp.where(block == 1, -1, jnp.where(block == 2, -2, jnp.where(block == 3, 1, jnp.where(block == 4, 2, 0))))
    flip = jnp.where(block >= 3, 1, 0)
    in_core = (core + flip + (col // 4) % 2) % 2
    ids = 8 * (dev // 2 + (1 - 2 * core) * step) + in_core * 4 + col % 4
    ids = jnp.where(block < 5, ids, -1)
    return jnp.where(wanted == ids, 1.0, 0.0).astype(BF16)


def correlate_kernel(dev_ref, partners_hbm, *refs):
    near_hbm, (recv_hbm, table_hbm, tw_hbm, near_out, far_out), refs = refs[:3], refs[3:8], refs[8:]
    near_refs, (recv_ref, table_ref, tw_ref, partners_ref), refs = refs[:3], refs[3:7], refs[7:]
    x_ref, u1_ref, u4_ref, u2_ref, z_ref, w_ref, p_ref, s1_ref, s2_ref, h_ref, o_ref, near_ref, far_ref, sems, out_sems = refs
    inputs = [*zip(near_hbm, near_refs), (recv_hbm, recv_ref)]
    moves = fetch([*inputs, (tw_hbm, tw_ref), (table_hbm, table_ref), (partners_hbm, partners_ref)], sems)
    x_ref[pl.ds(40 * STRIDE, 8 * STRIDE), :] = jnp.zeros((8 * STRIDE, LANES), F32)
    start = 0
    for move, ref in zip(moves, (*near_refs, recv_ref)):
        move.wait()
        start = NEAR if ref is recv_ref else start
        spread(x_ref, STRIDE, start, ref, ref.shape[0] // ROWS)
        start += ref.shape[0] // ROWS
    level = 0.1 * forward(x_ref, STRIDE, N, u1_ref, u4_ref, u2_ref, z_ref, table_ref, tw_ref, (moves[5], moves[4])) + 1e-6
    for chunk, (re, im) in enumerate(COLS):
        wr, wi = whitened(z_ref, level, re, im)
        for w in range(2):
            w_ref[w, :, re : re + LANES] = wr[w * N : w * N + NEAR].astype(BF16)
            w_ref[w, :, im : im + LANES] = wi[w * N : w * N + NEAR].astype(BF16)
        for i in range(4):
            sr = si = 0.0
            for w in range(2):
                at = w * N + NEAR
                fr, fi = wr[at : at + FAR], wi[at : at + FAR]
                br, bi = wr[w * N + i : w * N + i + 1], wi[w * N + i : w * N + i + 1]
                sr = sr + (fr * br + fi * bi)
                si = si + (fi * br - fr * bi)
            put(s1_ref, s2_ref, chunk, 64 + i * FAR, sr, si)
    moves[6].wait()
    picker = picked(dev_ref[0], partners_ref)
    for w in range(2):
        p_ref[w] = dot(picker, w_ref[w])
    for chunk, (re, im) in enumerate(COLS):
        own = [[w_ref[w, 0:16, k : k + LANES].astype(F32) for k in (re, im)] for w in range(2)]
        for c in range(4):
            sr = si = 0.0
            for w in range(2):
                pr, pi = (p_ref[w, c * 16 : (c + 1) * 16, k : k + LANES] for k in (re, im))
                ar, ai = own[w][0][c : c + 1], own[w][1][c : c + 1]
                sr = sr + (ar * pr + ai * pi)
                si = si + (ai * pr - ar * pi)
            put(s1_ref, s2_ref, chunk, c * 16, sr, si)
    backward(s1_ref, s2_ref, h_ref, PAIRS, table_ref, tw_ref)
    for lo in range(0, 64, 16):
        for part in range(2):
            for a, lag in enumerate(lags(h_ref, lo, 16, part)):
                at = 256 * a + LANES * part
                near_ref[lo : lo + 16, at : at + LANES] = lag.astype(BF16)
    outs = [pltpu.make_async_copy(near_ref, near_out, out_sems.at[0])]
    outs[0].start()
    for g in range(FAR // GROUP):
        for i in range(4):
            for part in range(2):
                for a, lag in enumerate(lags(h_ref, 64 + i * FAR + g * GROUP, GROUP, part)):
                    o_ref[pl.ds(g * GROUP * SLOT + (2 * a + part) * 4 + i, GROUP, stride=SLOT), :] = lag
        for s in range(g * GROUP, (g + 1) * GROUP):
            far_ref[pl.ds(s * 64, 64), :] = o_ref[pl.ds(s * SLOT, 64), :].astype(BF16)
        rows = pl.ds(g * GROUP * 64, GROUP * 64)
        outs.append(pltpu.make_async_copy(far_ref.at[rows, :], far_out.at[rows, :], out_sems.at[1 + g]))
        outs[-1].start()
    for out in outs:
        out.wait()


def vmem():
    return pl.BlockSpec(memory_space=pltpu.VMEM)


def smem():
    return pl.BlockSpec(memory_space=pltpu.SMEM)


def hbm():
    return pl.BlockSpec(memory_space=pltpu.HBM)


def like(*shape):
    return jax.ShapeDtypeStruct(shape, BF16)


def shards(records, partners, routes):
    table, twiddles = (jnp.asarray(x) for x in make_tables())
    members = lax.axis_size("dev")
    swap = [(d, d ^ 1) for d in range(members)]

    def toward(chips):
        pairs = [(d, d + (2 * chips if d % 2 == 0 else -2 * chips)) for d in range(members)]
        return [(s, t) for s, t in pairs if 0 <= t < members]

    raw = records.reshape(4, 2, 16, LANES).transpose(0, 2, 1, 3).reshape(4 * ROWS, LANES)
    outgoing = pl.pallas_call(
        select_kernel,
        out_shape=like(32 * ROWS, LANES),
        in_specs=[hbm(), hbm()],
        out_specs=vmem(),
        scratch_shapes=[
            pltpu.SMEM((2, 4), jnp.int32),
            pltpu.VMEM((4 * ROWS, LANES), BF16),
            pltpu.SemaphoreType.DMA((2,)),
        ],
        name="select",
    )(routes.T, raw)
    other = lax.ppermute(raw, "dev", swap)
    arrived = lax.all_to_all(outgoing.reshape(16, 2 * ROWS, LANES), "grp", 0, 0, tiled=True).reshape(32 * ROWS, LANES)

    chip = jnp.concatenate([raw, other], axis=0)
    one_side = lax.ppermute(chip, "dev", toward(1))
    two_side = lax.ppermute(chip, "dev", toward(2))
    side = jnp.concatenate([one_side, two_side], axis=0)
    far_side = lax.ppermute(side, "dev", swap)
    dev = lax.axis_index("dev").astype(jnp.int32).reshape(1)
    blocks = (chip, side, far_side)
    near, far = pl.pallas_call(
        correlate_kernel,
        out_shape=(like(64, NT), like(64 * FAR, LANES)),
        in_specs=[smem()] + [hbm()] * 7,
        out_specs=(hbm(), hbm()),
        scratch_shapes=[pltpu.VMEM(x.shape, BF16) for x in (*blocks, arrived, table)]
        + [
            pltpu.VMEM(twiddles.shape, F32),
            pltpu.SMEM((4, 16), jnp.int32),
            pltpu.VMEM((N * STRIDE, LANES), F32),
            pltpu.VMEM((2 * N, 256), BF16),
            pltpu.VMEM((2 * N, 512), BF16),
            pltpu.VMEM((6 * N, 512), BF16),
            pltpu.VMEM((2 * N, NT), F32),
            pltpu.VMEM((2, NEAR, NT), BF16),
            pltpu.VMEM((2, 64, NT), F32),
            pltpu.VMEM((2 * PAIRS, 256), BF16),
            pltpu.VMEM((3 * PAIRS, 512), BF16),
            pltpu.VMEM((PAIRS, NT), F32),
            pltpu.VMEM((FAR * SLOT, LANES), F32),
            pltpu.VMEM((64, NT), BF16),
            pltpu.VMEM((64 * FAR, LANES), BF16),
            pltpu.SemaphoreType.DMA((7,)),
            pltpu.SemaphoreType.DMA((1 + FAR // GROUP,)),
        ],
        compiler_params=pltpu.CompilerParams(vmem_limit_bytes=VMEM_LIMIT),
        name="correlate",
    )(dev, partners, *blocks, arrived, table, twiddles)
    far = far.reshape(32, 16, 4, LANES).transpose(0, 2, 1, 3).reshape(1, 1, 32, 4, NT)
    return (near.reshape(4, 16, NT), far)


def solution(mesh):
    placed = (P(("grp", "dev"), None, None), P(("grp", "dev"), None), P(("grp", "dev"), None))
    return jax.shard_map(
        shards,
        mesh=mesh,
        in_specs=placed,
        out_specs=(P(("grp", "dev"), None, None), P("grp", "dev", None, None, None)),
        check_vma=False,
    )
```

```python
import math

import jax
import jax.numpy as jnp
import numpy as np
from jax import lax
from jax.experimental import pallas as pl
from jax.experimental.pallas import tpu as pltpu
from jax.sharding import PartitionSpec as P

NT = 2048
BINS = 1024
LANES = 128
ROWS = 32
C = math.sqrt(0.5)
TURN = [(math.cos(math.pi * r / 8), math.sin(math.pi * r / 8)) for r in range(4)]
COLS = tuple((256 * m, 256 * m + 128) for m in range(8))
F32, BF16 = jnp.float32, jnp.bfloat16


def make_tables():
    b = np.arange(LANES)
    angle = b[:, None] * b[None, :] % LANES * (2.0 * np.pi / LANES)
    c, s = np.cos(angle), np.sin(angle)
    whole = np.block([[c, -s], [s, c]])
    c, s = c[:, :64], s[:, :64]
    o = np.zeros_like(c)
    ends = np.block([[c, o, -s, o], [o, c, o, -s], [o, s, o, c]])
    turn = np.arange(1, 9)[:, None] * b[None, :] * (2.0 * np.pi / NT)
    twiddles = np.concatenate([np.cos(turn), np.sin(turn)], axis=0).astype(np.float32)
    table = np.concatenate([whole, ends], axis=0)
    table = np.concatenate([table[:, :LANES], table[:, LANES:]], axis=0)
    return table.astype(np.float32).astype(jnp.bfloat16), twiddles


VMEM_LIMIT = 60 * 1024 * 1024


def dot(a, b):
    return jnp.dot(a, b, preferred_element_type=F32)


def fetch(pairs, sems):
    moves = [pltpu.make_async_copy(src, dst, sems.at[m]) for m, (src, dst) in enumerate(pairs)]
    for move in moves:
        move.start()
    return moves


def dot_t(a, b):
    return lax.dot_general(a, b, (((1,), (1,)), ((), ())), preferred_element_type=F32)


def tables(table_ref):
    side = table_ref.shape[0] // 2
    whole = jnp.concatenate([table_ref[0:256, :], table_ref[side : side + 256, :]], axis=1)
    ends = jnp.concatenate([table_ref[256:side, :], table_ref[side + 256 : 2 * side, :]], axis=1)
    return whole, ends


def eight(x):
    s = [x[a] + x[a + 4] for a in range(4)]
    d = [x[a] - x[a + 4] for a in range(4)]
    even, odd = s[0] + s[2], s[1] + s[3]
    diff, summ = C * (d[1] - d[3]), C * (d[1] + d[3])
    return even + odd, even - odd, ((d[0] + diff, -d[2] - summ), (s[0] - s[2], s[3] - s[1]), (d[0] - diff, d[2] - summ))


def select_kernel(routes_hbm, own_hbm, out_ref, routes_ref, own_ref, sems):
    for move in fetch([(routes_hbm, routes_ref), (own_hbm, own_ref)], sems):
        move.wait()
    for h in range(16):
        hit = [(routes_ref[0, i] == h) | (routes_ref[1, i] == h) for i in range(4)]
        count = sum(x.astype(jnp.int32) for x in hit)
        first = jnp.where(hit[0], 0, jnp.where(hit[1], 1, jnp.where(hit[2], 2, 3)))
        last = jnp.where(hit[3], 3, jnp.where(hit[2], 2, jnp.where(hit[1], 1, 0)))
        for k, pick in ((0, first), (1, last)):
            rows = own_ref[pl.ds(pl.multiple_of(pick * ROWS, ROWS), ROWS), :]
            out_ref[pl.ds((2 * h + k) * ROWS, ROWS), :] = jnp.where(count > k, rows, jnp.zeros_like(rows))


def spread(x_ref, stride, start, blk_ref, count):
    for c in range(count):
        x_ref[pl.ds((start + c) * stride, ROWS), :] = blk_ref[pl.ds(c * ROWS, ROWS), :].astype(F32)


def forward(x_ref, stride, n, one_ref, two_ref, z_ref, table_ref, tw_ref, moves):
    rows = 2 * n
    moves[1].wait()
    cos = [jnp.broadcast_to(tw_ref[m : m + 1, :], (16, LANES)) for m in range(8)]
    sin = [jnp.broadcast_to(tw_ref[m + 8 : m + 9, :], (16, LANES)) for m in range(8)]
    for w in range(2):
        for lo in range(0, n, 16):
            x = [x_ref[pl.ds(lo * stride + 2 * a + w, 16, stride=stride), :] for a in range(16)]
            e0, e4, e = eight(x[0::2])
            o0, o4, o = eight(x[1::2])
            at = pl.ds(w * n + lo, 16)
            last = e0 - o0
            one_ref[at, 0:128] = (e0 + o0).astype(BF16)
            one_ref[at, 128:256] = (last * cos[7]).astype(BF16)
            one_ref[at, 256:384] = (-last * sin[7]).astype(BF16)
            pairs = {4: (e4, -o4)}
            for r in (1, 2, 3):
                (er, ei), (br, bi), (c, s) = e[r - 1], o[r - 1], TURN[r]
                tr, ti = c * br + s * bi, c * bi - s * br
                pairs[r] = (er + tr, ei + ti)
                pairs[8 - r] = (er - tr, ti - ei)
            for r, (re, im) in pairs.items():
                at = pl.ds((r - 1) * rows + w * n + lo, 16)
                two_ref[at, 0:128] = (re * cos[r - 1] + im * sin[r - 1]).astype(BF16)
                two_ref[at, 128:256] = (im * cos[r - 1] - re * sin[r - 1]).astype(BF16)
    moves[0].wait()
    whole, ends = tables(table_ref)
    z_ref[:, 0:256] = dot(one_ref[...], ends)
    y = dot(two_ref[...], whole)
    for r in range(1, 8):
        z_ref[:, 256 * r : 256 * (r + 1)] = y[(r - 1) * rows : r * rows]
    total = None
    for re, im in COLS:
        zr, zi = z_ref[:, re : re + LANES], z_ref[:, im : im + LANES]
        energy = zr * zr + zi * zi
        total = energy if total is None else total + energy
    return jnp.sum(total, axis=1, keepdims=True) * (1.0 / BINS)


def backward(one_ref, two_ref, h_ref, n, table_ref, tw_ref):
    whole, ends = tables(table_ref)
    y = dot_t(one_ref[...], ends)
    h_ref[:, 0:128] = y[:, 0:128]
    h_ref[:, 128:256] = y[:, 128:256] * tw_ref[7:8, :] - y[:, 256:384] * tw_ref[15:16, :]
    y = dot_t(two_ref[...], whole)
    for r in range(1, 8):
        re, im = y[(r - 1) * n : r * n, 0:128], y[(r - 1) * n : r * n, 128:256]
        cos, sin = tw_ref[r - 1 : r, :], tw_ref[r + 7 : r + 8, :]
        h_ref[:, 256 * r : 256 * r + 128] = re * cos - im * sin
        h_ref[:, 256 * r + 128 : 256 * (r + 1)] = re * sin + im * cos


def whitened(z_ref, level, re, im):
    n = level.shape[0]
    zr, zi = z_ref[0:n, re : re + LANES], z_ref[0:n, im : im + LANES]
    scale = lax.rsqrt(zr * zr + zi * zi + level)
    return zr * scale, zi * scale


def put(one_ref, two_ref, chunk, lo, sr, si):
    n = sr.shape[0]
    sr, si = (sr * (1.0 / 64)).astype(BF16), (si * (1.0 / 64)).astype(BF16)
    if chunk == 0:
        one_ref[pl.ds(lo, n), 0:LANES] = sr
        one_ref[pl.ds(lo, n), LANES : 2 * LANES] = si
    else:
        rows = pl.ds((chunk - 1) * (two_ref.shape[0] // 7) + lo, n)
        two_ref[rows, 0:LANES] = sr
        two_ref[rows, LANES : 2 * LANES] = si


def eight_lags(p0, p4, a1, b1, a2, b2, a3, b3):
    even, odd = p0 + p4, p0 - p4
    plus, minus = even + a2, even - a2
    a13, b31 = a1 + a3, b3 - b1
    low, high = odd - b2, odd + b2
    t1, t3 = C * (a1 - b1 - a3 - b3), C * (a3 - b3 - a1 - b1)
    return (plus + a13, low + t1, minus + b31, high + t3, plus - a13, low - t1, minus - b31, high - t3)


def lags(h_ref, lo, n):
    h = [h_ref[lo : lo + n, LANES * m : LANES * (m + 1)] for m in range(16)]
    even, odd = [h[0] + h[1], h[8]], [h[0] - h[1], -h[9]]
    for r in (1, 2, 3):
        (ar, br), (al, bl), (c, s) = h[2 * r : 2 * r + 2], h[16 - 2 * r : 18 - 2 * r], TURN[r]
        da, sb = ar - al, br + bl
        even += [ar + al, br - bl]
        odd += [c * da - s * sb, s * da + c * sb]
    pairs = zip(eight_lags(*even), eight_lags(*odd))
    return [lag for pair in pairs for lag in pair]


NEAR, FAR, N = 48, 32, 80
STRIDE = 40
PAIRS, SLOT = 64 + 4 * FAR, 72
GROUP = 8


def picked(dev, partners_ref):
    core = dev % 2
    col = lax.broadcasted_iota(jnp.int32, (64, NEAR), 1)
    row = lax.broadcasted_iota(jnp.int32, (64, NEAR), 0)
    wanted = jnp.zeros((64, NEAR), jnp.int32)
    for c in range(4):
        for q in range(16):
            wanted = jnp.where(row == c * 16 + q, partners_ref[c, q] & 127, wanted)
    block = col // 8
    step = jnp.where(block == 1, -1, jnp.where(block == 2, -2, jnp.where(block == 3, 1, jnp.where(block == 4, 2, 0))))
    flip = jnp.where(block >= 3, 1, 0)
    in_core = (core + flip + (col // 4) % 2) % 2
    ids = 8 * (dev // 2 + (1 - 2 * core) * step) + in_core * 4 + col % 4
    ids = jnp.where(block < 5, ids, -1)
    return jnp.where(wanted == ids, 1.0, 0.0).astype(BF16)


def correlate_kernel(dev_ref, partners_hbm, *refs):
    near_hbm, (recv_hbm, table_hbm, tw_hbm, near_out, far_out), refs = refs[:3], refs[3:8], refs[8:]
    near_refs, (recv_ref, table_ref, tw_ref, partners_ref), refs = refs[:3], refs[3:7], refs[7:]
    x_ref, u1_ref, u2_ref, z_ref, w_ref, p_ref, s1_ref, s2_ref, h_ref, o_ref, near_ref, far_ref, sems, out_sems = refs
    inputs = [*zip(near_hbm, near_refs), (recv_hbm, recv_ref)]
    moves = fetch([*inputs, (tw_hbm, tw_ref), (table_hbm, table_ref), (partners_hbm, partners_ref)], sems)
    x_ref[pl.ds(40 * STRIDE, 8 * STRIDE), :] = jnp.zeros((8 * STRIDE, LANES), F32)
    start = 0
    for move, ref in zip(moves, (*near_refs, recv_ref)):
        move.wait()
        start = NEAR if ref is recv_ref else start
        spread(x_ref, STRIDE, start, ref, ref.shape[0] // ROWS)
        start += ref.shape[0] // ROWS
    level = 0.1 * forward(x_ref, STRIDE, N, u1_ref, u2_ref, z_ref, table_ref, tw_ref, (moves[5], moves[4])) + 1e-6
    for chunk, (re, im) in enumerate(COLS):
        wr, wi = whitened(z_ref, level, re, im)
        for w in range(2):
            w_ref[w, :, re : re + LANES] = wr[w * N : w * N + NEAR].astype(BF16)
            w_ref[w, :, im : im + LANES] = wi[w * N : w * N + NEAR].astype(BF16)
        for i in range(4):
            sr = si = 0.0
            for w in range(2):
                at = w * N + NEAR
                fr, fi = wr[at : at + FAR], wi[at : at + FAR]
                br, bi = wr[w * N + i : w * N + i + 1], wi[w * N + i : w * N + i + 1]
                sr = sr + (fr * br + fi * bi)
                si = si + (fi * br - fr * bi)
            put(s1_ref, s2_ref, chunk, 64 + i * FAR, sr, si)
    moves[6].wait()
    picker = picked(dev_ref[0], partners_ref)
    for w in range(2):
        p_ref[w] = dot(picker, w_ref[w])
    for chunk, (re, im) in enumerate(COLS):
        own = [[w_ref[w, 0:16, k : k + LANES].astype(F32) for k in (re, im)] for w in range(2)]
        for c in range(4):
            sr = si = 0.0
            for w in range(2):
                pr, pi = (p_ref[w, c * 16 : (c + 1) * 16, k : k + LANES] for k in (re, im))
                ar, ai = own[w][0][c : c + 1], own[w][1][c : c + 1]
                sr = sr + (ar * pr + ai * pi)
                si = si + (ai * pr - ar * pi)
            put(s1_ref, s2_ref, chunk, c * 16, sr, si)
    backward(s1_ref, s2_ref, h_ref, PAIRS, table_ref, tw_ref)
    for lo in range(0, 64, 16):
        for a, lag in enumerate(lags(h_ref, lo, 16)):
            near_ref[lo : lo + 16, LANES * a : LANES * (a + 1)] = lag.astype(BF16)
    outs = [pltpu.make_async_copy(near_ref, near_out, out_sems.at[0])]
    outs[0].start()
    for g in range(FAR // GROUP):
        for i in range(4):
            for a, lag in enumerate(lags(h_ref, 64 + i * FAR + g * GROUP, GROUP)):
                o_ref[pl.ds(g * GROUP * SLOT + a * 4 + i, GROUP, stride=SLOT), :] = lag
        for s in range(g * GROUP, (g + 1) * GROUP):
            far_ref[pl.ds(s * 64, 64), :] = o_ref[pl.ds(s * SLOT, 64), :].astype(BF16)
        rows = pl.ds(g * GROUP * 64, GROUP * 64)
        outs.append(pltpu.make_async_copy(far_ref.at[rows, :], far_out.at[rows, :], out_sems.at[1 + g]))
        outs[-1].start()
    for out in outs:
        out.wait()


def vmem():
    return pl.BlockSpec(memory_space=pltpu.VMEM)


def smem():
    return pl.BlockSpec(memory_space=pltpu.SMEM)


def hbm():
    return pl.BlockSpec(memory_space=pltpu.HBM)


def like(*shape):
    return jax.ShapeDtypeStruct(shape, BF16)


def shards(records, partners, routes):
    table, twiddles = (jnp.asarray(x) for x in make_tables())
    members = lax.axis_size("dev")
    swap = [(d, d ^ 1) for d in range(members)]

    def toward(chips):
        pairs = [(d, d + (2 * chips if d % 2 == 0 else -2 * chips)) for d in range(members)]
        return [(s, t) for s, t in pairs if 0 <= t < members]

    raw = records.reshape(4, 2, 16, LANES).transpose(0, 2, 1, 3).reshape(4 * ROWS, LANES)
    outgoing = pl.pallas_call(
        select_kernel,
        out_shape=like(32 * ROWS, LANES),
        in_specs=[hbm(), hbm()],
        out_specs=vmem(),
        scratch_shapes=[
            pltpu.SMEM((2, 4), jnp.int32),
            pltpu.VMEM((4 * ROWS, LANES), BF16),
            pltpu.SemaphoreType.DMA((2,)),
        ],
        name="select",
    )(routes.T, raw)
    other = lax.ppermute(raw, "dev", swap)
    arrived = lax.all_to_all(outgoing.reshape(16, 2 * ROWS, LANES), "grp", 0, 0, tiled=True).reshape(32 * ROWS, LANES)

    chip = jnp.concatenate([raw, other], axis=0)
    two_side = lax.ppermute(chip, "dev", toward(2))
    one_side = lax.ppermute(chip, "dev", toward(1))
    side = jnp.concatenate([one_side, two_side], axis=0)
    far_side = lax.ppermute(side, "dev", swap)
    dev = lax.axis_index("dev").astype(jnp.int32).reshape(1)
    blocks = (chip, side, far_side)
    near, far = pl.pallas_call(
        correlate_kernel,
        out_shape=(like(64, NT), like(64 * FAR, LANES)),
        in_specs=[smem()] + [hbm()] * 7,
        out_specs=(hbm(), hbm()),
        scratch_shapes=[pltpu.VMEM(x.shape, BF16) for x in (*blocks, arrived, table)]
        + [
            pltpu.VMEM(twiddles.shape, F32),
            pltpu.SMEM((4, 16), jnp.int32),
            pltpu.VMEM((N * STRIDE, LANES), F32),
            pltpu.VMEM((2 * N, 384), BF16),
            pltpu.VMEM((14 * N, 256), BF16),
            pltpu.VMEM((2 * N, NT), F32),
            pltpu.VMEM((2, NEAR, NT), BF16),
            pltpu.VMEM((2, 64, NT), F32),
            pltpu.VMEM((PAIRS, 256), BF16),
            pltpu.VMEM((7 * PAIRS, 256), BF16),
            pltpu.VMEM((PAIRS, NT), F32),
            pltpu.VMEM((FAR * SLOT, LANES), F32),
            pltpu.VMEM((64, NT), BF16),
            pltpu.VMEM((64 * FAR, LANES), BF16),
            pltpu.SemaphoreType.DMA((7,)),
            pltpu.SemaphoreType.DMA((1 + FAR // GROUP,)),
        ],
        compiler_params=pltpu.CompilerParams(vmem_limit_bytes=VMEM_LIMIT),
        name="correlate",
    )(dev, partners, *blocks, arrived, table, twiddles)
    far = far.reshape(32, 16, 4, LANES).transpose(0, 2, 1, 3).reshape(1, 1, 32, 4, NT)
    return (near.reshape(4, 16, NT), far)


def solution(mesh):
    placed = (P(("grp", "dev"), None, None), P(("grp", "dev"), None), P(("grp", "dev"), None))
    return jax.shard_map(
        shards,
        mesh=mesh,
        in_specs=placed,
        out_specs=(P(("grp", "dev"), None, None), P("grp", "dev", None, None, None)),
        check_vma=False,
    )
```

```python
import math

import jax
import jax.numpy as jnp
import numpy as np
from jax import lax
from jax.experimental import pallas as pl
from jax.experimental.pallas import tpu as pltpu
from jax.sharding import PartitionSpec as P

NT = 2048
BINS = 1024
LANES = 128
ROWS = 32
C = math.sqrt(0.5)
TURN = [(math.cos(math.pi * r / 8), math.sin(math.pi * r / 8)) for r in range(4)]
COLS = tuple((256 * m, 256 * m + 128) for m in range(8))
F32, BF16 = jnp.float32, jnp.bfloat16


def make_tables():
    b = np.arange(LANES)
    angle = b[:, None] * b[None, :] % LANES * (2.0 * np.pi / LANES)
    c, s = np.cos(angle), np.sin(angle)
    whole = np.block([[c, -s], [s, c]])
    c, s = c[:, :64], s[:, :64]
    o = np.zeros_like(c)
    ends = np.block([[c, o, -s, o], [o, c, o, -s], [o, s, o, c]])
    turn = np.arange(1, 9)[:, None] * b[None, :] * (2.0 * np.pi / NT)
    twiddles = np.concatenate([np.cos(turn), np.sin(turn)], axis=0).astype(np.float32)
    table = np.concatenate([whole, ends], axis=0)
    table = np.concatenate([table[:, :LANES], table[:, LANES:]], axis=0)
    return table.astype(np.float32).astype(jnp.bfloat16), twiddles


VMEM_LIMIT = 20 * 1024 * 1024


def dot(a, b):
    return jnp.dot(a, b, preferred_element_type=F32)


def fetch(pairs, sems):
    moves = [pltpu.make_async_copy(src, dst, sems.at[m]) for m, (src, dst) in enumerate(pairs)]
    for move in moves:
        move.start()
    return moves


def dot_t(a, b):
    return lax.dot_general(a, b, (((1,), (1,)), ((), ())), preferred_element_type=F32)


def tables(table_ref):
    side = table_ref.shape[0] // 2
    whole = jnp.concatenate([table_ref[0:256, :], table_ref[side : side + 256, :]], axis=1)
    ends = jnp.concatenate([table_ref[256:side, :], table_ref[side + 256 : 2 * side, :]], axis=1)
    return whole, ends


def eight(x):
    s = [x[a] + x[a + 4] for a in range(4)]
    d = [x[a] - x[a + 4] for a in range(4)]
    even, odd = s[0] + s[2], s[1] + s[3]
    diff, summ = C * (d[1] - d[3]), C * (d[1] + d[3])
    return even + odd, even - odd, ((d[0] + diff, -d[2] - summ), (s[0] - s[2], s[3] - s[1]), (d[0] - diff, d[2] - summ))


def select_kernel(routes_hbm, own_hbm, out_ref, routes_ref, own_ref, sems):
    for move in fetch([(routes_hbm, routes_ref), (own_hbm, own_ref)], sems):
        move.wait()
    for h in range(16):
        hit = [(routes_ref[0, i] == h) | (routes_ref[1, i] == h) for i in range(4)]
        count = sum(x.astype(jnp.int32) for x in hit)
        first = jnp.where(hit[0], 0, jnp.where(hit[1], 1, jnp.where(hit[2], 2, 3)))
        last = jnp.where(hit[3], 3, jnp.where(hit[2], 2, jnp.where(hit[1], 1, 0)))
        for k, pick in ((0, first), (1, last)):
            rows = own_ref[pl.ds(pl.multiple_of(pick * ROWS, ROWS), ROWS), :]
            out_ref[pl.ds((2 * h + k) * ROWS, ROWS), :] = jnp.where(count > k, rows, jnp.zeros_like(rows))


def spread(x_ref, stride, start, blk_ref, count):
    for c in range(count):
        x_ref[pl.ds((start + c) * stride, ROWS), :] = blk_ref[pl.ds(c * ROWS, ROWS), :].astype(F32)


def forward(x_ref, stride, n, one_ref, two_ref, z_ref, table_ref, tw_ref, moves):
    rows = 2 * n
    moves[1].wait()
    cos = [jnp.broadcast_to(tw_ref[m : m + 1, :], (16, LANES)) for m in range(8)]
    sin = [jnp.broadcast_to(tw_ref[m + 8 : m + 9, :], (16, LANES)) for m in range(8)]
    for w in range(2):
        for lo in range(0, n, 16):
            x = [x_ref[pl.ds(lo * stride + 2 * a + w, 16, stride=stride), :] for a in range(16)]
            e0, e4, e = eight(x[0::2])
            o0, o4, o = eight(x[1::2])
            at = pl.ds(w * n + lo, 16)
            last = e0 - o0
            one_ref[at, 0:128] = (e0 + o0).astype(BF16)
            one_ref[at, 128:256] = (last * cos[7]).astype(BF16)
            one_ref[at, 256:384] = (-last * sin[7]).astype(BF16)
            pairs = {4: (e4, -o4)}
            for r in (1, 2, 3):
                (er, ei), (br, bi), (c, s) = e[r - 1], o[r - 1], TURN[r]
                tr, ti = c * br + s * bi, c * bi - s * br
                pairs[r] = (er + tr, ei + ti)
                pairs[8 - r] = (er - tr, ti - ei)
            for r, (re, im) in pairs.items():
                at = pl.ds((r - 1) * rows + w * n + lo, 16)
                two_ref[at, 0:128] = (re * cos[r - 1] + im * sin[r - 1]).astype(BF16)
                two_ref[at, 128:256] = (im * cos[r - 1] - re * sin[r - 1]).astype(BF16)
    moves[0].wait()
    whole, ends = tables(table_ref)
    z_ref[:, 0:256] = dot(one_ref[...], ends)
    for r in range(1, 8):
        z_ref[:, 256 * r : 256 * (r + 1)] = dot(two_ref[pl.ds((r - 1) * rows, rows), :], whole)
    total = None
    for re, im in COLS:
        zr, zi = z_ref[:, re : re + LANES], z_ref[:, im : im + LANES]
        energy = zr * zr + zi * zi
        total = energy if total is None else total + energy
    return jnp.sum(total, axis=1, keepdims=True) * (1.0 / BINS)


def backward(one_ref, two_ref, h_ref, n, table_ref, tw_ref):
    whole, ends = tables(table_ref)
    y = dot_t(one_ref[...], ends)
    h_ref[:, 0:128] = y[:, 0:128]
    h_ref[:, 128:256] = y[:, 128:256] * tw_ref[7:8, :] - y[:, 256:384] * tw_ref[15:16, :]
    c, s = whole[0:LANES, 0:LANES], whole[LANES:256, 0:LANES]
    back = jnp.concatenate([jnp.concatenate([c, s], axis=1), jnp.concatenate([-s, c], axis=1)], axis=0)
    for r in range(1, 8):
        y = dot(two_ref[pl.ds((r - 1) * n, n), :], back)
        re, im = y[:, 0:128], y[:, 128:256]
        cos, sin = tw_ref[r - 1 : r, :], tw_ref[r + 7 : r + 8, :]
        h_ref[:, 256 * r : 256 * r + 128] = re * cos - im * sin
        h_ref[:, 256 * r + 128 : 256 * (r + 1)] = re * sin + im * cos


def whitened(z_ref, level, re, im):
    n = level.shape[0]
    zr, zi = z_ref[0:n, re : re + LANES], z_ref[0:n, im : im + LANES]
    scale = lax.rsqrt(zr * zr + zi * zi + level)
    return zr * scale, zi * scale


def put(one_ref, two_ref, chunk, lo, sr, si):
    n = sr.shape[0]
    sr, si = (sr * (1.0 / 64)).astype(BF16), (si * (1.0 / 64)).astype(BF16)
    if chunk == 0:
        one_ref[pl.ds(lo, n), 0:LANES] = sr
        one_ref[pl.ds(lo, n), LANES : 2 * LANES] = si
    else:
        rows = pl.ds((chunk - 1) * (two_ref.shape[0] // 7) + lo, n)
        two_ref[rows, 0:LANES] = sr
        two_ref[rows, LANES : 2 * LANES] = si


def eight_lags(p0, p4, a1, b1, a2, b2, a3, b3):
    even, odd = p0 + p4, p0 - p4
    plus, minus = even + a2, even - a2
    a13, b31 = a1 + a3, b3 - b1
    low, high = odd - b2, odd + b2
    t1, t3 = C * (a1 - b1 - a3 - b3), C * (a3 - b3 - a1 - b1)
    return (plus + a13, low + t1, minus + b31, high + t3, plus - a13, low - t1, minus - b31, high - t3)


def lags(h_ref, lo, n):
    h = [h_ref[lo : lo + n, LANES * m : LANES * (m + 1)] for m in range(16)]
    even, odd = [h[0] + h[1], h[8]], [h[0] - h[1], -h[9]]
    for r in (1, 2, 3):
        (ar, br), (al, bl), (c, s) = h[2 * r : 2 * r + 2], h[16 - 2 * r : 18 - 2 * r], TURN[r]
        da, sb = ar - al, br + bl
        even += [ar + al, br - bl]
        odd += [c * da - s * sb, s * da + c * sb]
    pairs = zip(eight_lags(*even), eight_lags(*odd))
    return [lag for pair in pairs for lag in pair]


NEAR, FAR, N = 48, 32, 80
STRIDE = 40
PAIRS, SLOT = 64 + 4 * FAR, 72
GROUP = 8


def picked(dev, partners_ref):
    core = dev % 2
    col = lax.broadcasted_iota(jnp.int32, (64, NEAR), 1)
    row = lax.broadcasted_iota(jnp.int32, (64, NEAR), 0)
    wanted = jnp.zeros((64, NEAR), jnp.int32)
    for c in range(4):
        for q in range(16):
            wanted = jnp.where(row == c * 16 + q, partners_ref[c, q] & 127, wanted)
    block = col // 8
    step = jnp.where(block == 1, -1, jnp.where(block == 2, -2, jnp.where(block == 3, 1, jnp.where(block == 4, 2, 0))))
    flip = jnp.where(block >= 3, 1, 0)
    in_core = (core + flip + (col // 4) % 2) % 2
    ids = 8 * (dev // 2 + (1 - 2 * core) * step) + in_core * 4 + col % 4
    ids = jnp.where(block < 5, ids, -1)
    return jnp.where(wanted == ids, 1.0, 0.0).astype(BF16)


def correlate_kernel(dev_ref, partners_hbm, *refs):
    near_hbm, (recv_hbm, table_hbm, tw_hbm, near_out, far_out), refs = refs[:3], refs[3:8], refs[8:]
    near_refs, (recv_ref, table_ref, tw_ref, partners_ref), refs = refs[:3], refs[3:7], refs[7:]
    x_ref, u1_ref, u2_ref, z_ref, w_ref, p_ref, s1_ref, s2_ref, h_ref, o_ref, near_ref, far_ref, sems, out_sems = refs
    inputs = [*zip(near_hbm, near_refs), (recv_hbm, recv_ref)]
    moves = fetch([*inputs, (tw_hbm, tw_ref), (table_hbm, table_ref), (partners_hbm, partners_ref)], sems)
    x_ref[pl.ds(40 * STRIDE, 8 * STRIDE), :] = jnp.zeros((8 * STRIDE, LANES), F32)
    start = 0
    for move, ref in zip(moves, (*near_refs, recv_ref)):
        move.wait()
        start = NEAR if ref is recv_ref else start
        spread(x_ref, STRIDE, start, ref, ref.shape[0] // ROWS)
        start += ref.shape[0] // ROWS
    level = 0.1 * forward(x_ref, STRIDE, N, u1_ref, u2_ref, z_ref, table_ref, tw_ref, (moves[5], moves[4])) + 1e-6
    for chunk, (re, im) in enumerate(COLS):
        wr, wi = whitened(z_ref, level, re, im)
        for w in range(2):
            w_ref[w, :, re : re + LANES] = wr[w * N : w * N + NEAR].astype(BF16)
            w_ref[w, :, im : im + LANES] = wi[w * N : w * N + NEAR].astype(BF16)
        for i in range(4):
            sr = si = 0.0
            for w in range(2):
                at = w * N + NEAR
                fr, fi = wr[at : at + FAR], wi[at : at + FAR]
                br, bi = wr[w * N + i : w * N + i + 1], wi[w * N + i : w * N + i + 1]
                sr = sr + (fr * br + fi * bi)
                si = si + (fi * br - fr * bi)
            put(s1_ref, s2_ref, chunk, 64 + i * FAR, sr, si)
    moves[6].wait()
    picker = picked(dev_ref[0], partners_ref)
    for w in range(2):
        p_ref[w] = dot(picker, w_ref[w])
    for chunk, (re, im) in enumerate(COLS):
        own = [[w_ref[w, 0:16, k : k + LANES].astype(F32) for k in (re, im)] for w in range(2)]
        for c in range(4):
            sr = si = 0.0
            for w in range(2):
                pr, pi = (p_ref[w, c * 16 : (c + 1) * 16, k : k + LANES] for k in (re, im))
                ar, ai = own[w][0][c : c + 1], own[w][1][c : c + 1]
                sr = sr + (ar * pr + ai * pi)
                si = si + (ai * pr - ar * pi)
            put(s1_ref, s2_ref, chunk, c * 16, sr, si)
    backward(s1_ref, s2_ref, h_ref, PAIRS, table_ref, tw_ref)
    for lo in range(0, 64, 16):
        for a, lag in enumerate(lags(h_ref, lo, 16)):
            near_ref[lo : lo + 16, LANES * a : LANES * (a + 1)] = lag.astype(BF16)
    outs = [pltpu.make_async_copy(near_ref, near_out, out_sems.at[0])]
    outs[0].start()
    for g in range(FAR // GROUP):
        for i in range(4):
            for a, lag in enumerate(lags(h_ref, 64 + i * FAR + g * GROUP, GROUP)):
                o_ref[pl.ds(g * GROUP * SLOT + a * 4 + i, GROUP, stride=SLOT), :] = lag
        for s in range(g * GROUP, (g + 1) * GROUP):
            far_ref[pl.ds(s * 64, 64), :] = o_ref[pl.ds(s * SLOT, 64), :].astype(BF16)
        rows = pl.ds(g * GROUP * 64, GROUP * 64)
        outs.append(pltpu.make_async_copy(far_ref.at[rows, :], far_out.at[rows, :], out_sems.at[1 + g]))
        outs[-1].start()
    for out in outs:
        out.wait()


def vmem():
    return pl.BlockSpec(memory_space=pltpu.VMEM)


def smem():
    return pl.BlockSpec(memory_space=pltpu.SMEM)


def hbm():
    return pl.BlockSpec(memory_space=pltpu.HBM)


def like(*shape):
    return jax.ShapeDtypeStruct(shape, BF16)


def shards(records, partners, routes):
    table, twiddles = (jnp.asarray(x) for x in make_tables())
    members = lax.axis_size("dev")
    swap = [(d, d ^ 1) for d in range(members)]

    def toward(chips):
        pairs = [(d, d + (2 * chips if d % 2 == 0 else -2 * chips)) for d in range(members)]
        return [(s, t) for s, t in pairs if 0 <= t < members]

    raw = records.reshape(4, 2, 16, LANES).transpose(0, 2, 1, 3).reshape(4 * ROWS, LANES)
    outgoing = pl.pallas_call(
        select_kernel,
        out_shape=like(32 * ROWS, LANES),
        in_specs=[hbm(), hbm()],
        out_specs=vmem(),
        scratch_shapes=[
            pltpu.SMEM((2, 4), jnp.int32),
            pltpu.VMEM((4 * ROWS, LANES), BF16),
            pltpu.SemaphoreType.DMA((2,)),
        ],
        name="select",
    )(routes.T, raw)
    other = lax.ppermute(raw, "dev", swap)
    arrived = lax.all_to_all(outgoing.reshape(16, 2 * ROWS, LANES), "grp", 0, 0, tiled=True).reshape(32 * ROWS, LANES)

    chip = jnp.concatenate([raw, other], axis=0)
    two_side = lax.ppermute(chip, "dev", toward(2))
    one_side = lax.ppermute(chip, "dev", toward(1))
    side = jnp.concatenate([one_side, two_side], axis=0)
    far_side = lax.ppermute(side, "dev", swap)
    dev = lax.axis_index("dev").astype(jnp.int32).reshape(1)
    blocks = (chip, side, far_side)
    near, far = pl.pallas_call(
        correlate_kernel,
        out_shape=(like(64, NT), like(64 * FAR, LANES)),
        in_specs=[smem()] + [hbm()] * 7,
        out_specs=(hbm(), hbm()),
        scratch_shapes=[pltpu.VMEM(x.shape, BF16) for x in (*blocks, arrived, table)]
        + [
            pltpu.VMEM(twiddles.shape, F32),
            pltpu.SMEM((4, 16), jnp.int32),
            pltpu.VMEM((N * STRIDE, LANES), F32),
            pltpu.VMEM((2 * N, 384), BF16),
            pltpu.VMEM((14 * N, 256), BF16),
            pltpu.VMEM((2 * N, NT), F32),
            pltpu.VMEM((2, NEAR, NT), BF16),
            pltpu.VMEM((2, 64, NT), F32),
            pltpu.VMEM((PAIRS, 256), BF16),
            pltpu.VMEM((7 * PAIRS, 256), BF16),
            pltpu.VMEM((PAIRS, NT), F32),
            pltpu.VMEM((FAR * SLOT, LANES), F32),
            pltpu.VMEM((64, NT), BF16),
            pltpu.VMEM((64 * FAR, LANES), BF16),
            pltpu.SemaphoreType.DMA((7,)),
            pltpu.SemaphoreType.DMA((1 + FAR // GROUP,)),
        ],
        compiler_params=pltpu.CompilerParams(vmem_limit_bytes=VMEM_LIMIT),
        name="correlate",
    )(dev, partners, *blocks, arrived, table, twiddles)
    far = far.reshape(32, 16, 4, LANES).transpose(0, 2, 1, 3).reshape(1, 1, 32, 4, NT)
    return (near.reshape(4, 16, NT), far)


def solution(mesh):
    placed = (P(("grp", "dev"), None, None), P(("grp", "dev"), None), P(("grp", "dev"), None))
    return jax.shard_map(
        shards,
        mesh=mesh,
        in_specs=placed,
        out_specs=(P(("grp", "dev"), None, None), P("grp", "dev", None, None, None)),
        check_vma=False,
    )
```
